32 devices in a mesh: row: 8 (over z, x), col: 4 (over y, core).
Axes of the slice: x: 2, y: 2, z: 4, core: 2. Of those that a mesh axis runs over, the one named last changes fastest.
Arguments:
- trailing: bfloat16 [16384, 2048], P('row', 'col'), may hold values from -6 to 6
- panel: float32 [16384, 256], P(('row', 'col')), may hold values from -1 to 1
- diag_inverse: float32 [256, 256], P(None, 'col'), may hold values from -1 to 2, as said below
Outputs:
- updated: bfloat16 [16384, 2048], P('row', 'col')
The draws below stay inside these ranges and needn't reach their ends.
Inputs may be any that keep to these rules, and one draw needn't show every extreme that they name: `diag_inverse`: lower triangular with a positive diagonal.
All inputs are finite; a program needn't handle non-finite values.
Results may differ from the reference program's by a relative error of at most 0.0051.
Values may be sent and summed in bfloat16 or wider, within the bound.
No kernel may reach another device: no remote copies, remote signals or barrier semaphores. Data moves between devices by JAX's collectives and lax.ppermute only.
A program may use at most 64 MiB of HBM per device.

```python
import math
import jax
import jax.numpy as jnp
from jax import lax

NB = 256
SBLK = 2
ROWS_DEV = 2048
ORDER = 16384
SLAB = 2048
N_ROW = 8
N_COL = 4


def draw_diag_inverse(key, part):
    key_off, key_diag = jax.random.split(key)
    row_ids = lax.broadcasted_iota(jnp.int32, (NB, NB), 0)
    col_ids = lax.broadcasted_iota(jnp.int32, (NB, NB), 1)
    lower_part = jnp.clip(jax.random.normal(key_off, (NB, NB), jnp.float32), -4.0, 4.0) / math.sqrt(NB)
    diagonal = jax.random.uniform(key_diag, (NB, NB), jnp.float32, 1.0, 2.0)
    return jnp.where(row_ids == col_ids, diagonal, jnp.where(row_ids > col_ids, lower_part, 0.0))


def block_levels(stream_key, extent, shards, low, high):
    def one(dim, shards_of):
        steps = jax.random.uniform(jax.random.fold_in(jax.random.fold_in(stream_key, 6), dim), (shards_of,), jnp.float32, low / len(shards), high / len(shards))
        return jnp.repeat(jnp.exp(steps), extent[dim] // shards_of).reshape((-1,) + (1,) * (len(extent) - dim - 1))

    gain = one(*shards[0])
    for cut in shards[1:]:
        gain = gain * one(*cut)
    return gain


def scatter_about(own_key, shape, scale, most, cuts=(), dtype=jnp.bfloat16):
    values = jax.random.normal(own_key, shape, jnp.float32) * scale
    if len(cuts) > 0:
        values = block_levels(own_key, shape, cuts, -0.22, 0.18) * values
    return jnp.clip(values, min=-most, max=most).astype(dtype)


def setup_inputs(seed: int = 0) -> dict:
    key_list = jax.random.split(jax.random.key(seed), 4)
    trailing = scatter_about(key_list[0], (ORDER, SLAB), 1.0, 6.0, ((0, 8), (1, 4)))
    panel = scatter_about(key_list[1], (ORDER, NB), 0.17, 1.0, ((0, 32),), jnp.float32)
    diag_inverse = draw_diag_inverse(jax.random.fold_in(key_list[3], 71), 0)
    return {"trailing": trailing, "panel": panel, "diag_inverse": diag_inverse}


def reference(trailing, panel, diag_inverse):
    solved = jnp.dot(panel, diag_inverse.T, precision=lax.Precision.HIGHEST, preferred_element_type=jnp.float32).astype(jnp.bfloat16)
    grouped = solved.reshape(N_ROW, ROWS_DEV, NB)
    tops = grouped[:SBLK * N_COL, :NB, :]
    mirror = tops.reshape(SBLK, N_COL, NB, NB).transpose(1, 0, 2, 3).reshape(SLAB, NB)
    slabs = trailing.reshape(N_ROW, ROWS_DEV, SLAB)

    def one_block(pair):
        slab_rows, solved_rows = pair
        product = jnp.dot(solved_rows, mirror.T, preferred_element_type=jnp.float32)
        return (slab_rows.astype(jnp.float32) - product).astype(jnp.bfloat16)

    result = lax.map(one_block, (slabs, grouped))
    return result.reshape(ORDER, SLAB)
```

```python
import jax
import jax.numpy as jnp
from jax import lax
from jax.experimental import pallas as pl
from jax.experimental.pallas import tpu as pltpu
from jax.sharding import PartitionSpec as P

NB = 256
SBLK = 2
SCALE = 32768.0
AXES = ("row", "col")
F32, F16, BF16 = jnp.float32, jnp.float16, jnp.bfloat16


def from_root(value, axis, source):
    kept = jnp.where(lax.axis_index(axis) == source, value, 0).astype(value.dtype)
    return lax.psum(kept, axis)


def solve_rows(rows_in, inverse):
    return lax.dot_general(
        rows_in,
        inverse,
        (((1,), (1,)), ((), ())),
        precision=lax.Precision.HIGHEST,
        preferred_element_type=F32,
    ).astype(BF16)


def local_any(trailing, panel, diag_inverse):
    inverse = lax.all_gather(diag_inverse, "col", axis=1, tiled=True)
    raw_rows = lax.all_gather(panel, "col", axis=0, tiled=True)
    solved = solve_rows(raw_rows, inverse)
    top_block = solved[:NB]
    col_index = lax.axis_index("col")
    col_count = lax.axis_size("col")
    pieces = []
    for section in range(SBLK):
        pieces.append(from_root(top_block, "row", col_index + section * col_count))
    mirror = jnp.concatenate(pieces, 0)
    update = lax.dot_general(
        solved, mirror, (((1,), (1,)), ((), ())), preferred_element_type=F32
    )
    return (trailing.astype(F32) - update).astype(BF16)


def dev(z, x, y, k):
    return (z * 2 + x) * 4 + y * 2 + k


ALL = [(z, x, y, k) for z in range(4) for x in range(2) for y in range(2) for k in range(2)]
CORE = [(dev(z, x, y, k), dev(z, x, y, 1 - k)) for z, x, y, k in ALL]
ACROSS = [(dev(z, x, y, k), dev(z, x, 1 - y, k)) for z, x, y, k in ALL]


def spread(j):
    pairs = []
    for z in range(4):
        for x in range(2):
            pairs.append((dev(z, x, 0, 1 - x), dev(z ^ j, x, z % 2, x)))
            for y in range(2):
                pairs.append((dev(z, x, y, x), dev(z, x, y, 1 - x)))
            back = 0 if (z ^ j) % 2 == 1 else 1
            pairs.append((dev(z, x, 1, 1 - x), dev(z, x, back, x)))
    return pairs


ASIDE = [
    (dev(z, x, y, k), dev(z, 1 - x, y, k) if k == x else dev(z, x, y, 1 - k))
    for z, x, y, k in ALL
]


def send(value, pairs):
    return lax.ppermute(value, AXES, pairs)


def split(value):
    high = value.astype(BF16)
    return high, (value - high.astype(F32)).astype(BF16)


def mul(a, b):
    return jnp.dot(a, b, preferred_element_type=F32)


def solve(rows, lt_hi, lt_lo):
    hi, lo = split(rows)
    return (mul(hi, lt_hi) + (mul(hi, lt_lo) + mul(lo, lt_hi))).astype(BF16)


def early_kernel(c_ref, own_ref, mate_ref, l0, l1, l2, l3, s_ref, hi_ref, lo_ref, lt_ref):
    c = c_ref[0]
    for i, block in enumerate((l0, l1, l2, l3)):
        at = pl.multiple_of((c ^ i) * 64, 64)
        lt_ref[pl.ds(at, 64), :] = block[...]
    hi, lo = split(lt_ref[...])
    hi_ref[...] = hi
    lo_ref[...] = lo
    s_ref[0] = solve(own_ref[...], hi, lo)
    s_ref[1] = solve(mate_ref[...], hi, lo)


def early(c, own, mate, blocks):
    vmem = pl.BlockSpec(memory_space=pltpu.VMEM)
    n = own.shape[0]
    return pl.pallas_call(
        early_kernel,
        out_shape=(
            jax.ShapeDtypeStruct((2, n, NB), BF16),
            jax.ShapeDtypeStruct((NB, NB), BF16),
            jax.ShapeDtypeStruct((NB, NB), BF16),
        ),
        in_specs=[pl.BlockSpec(memory_space=pltpu.SMEM)] + [vmem] * 6,
        out_specs=(vmem, vmem, vmem),
        scratch_shapes=[pltpu.VMEM((NB, NB), F32)],
        compiler_params=pltpu.CompilerParams(vmem_limit_bytes=24 * 1024 * 1024),
    )(c, own, mate, *blocks)


def final_kernel(c_ref, t_ref, s_ref, y0, y1, ky0, ky1, ta, tb, hi_ref, lo_ref, o_ref, m_ref, w_ref):
    i = pl.program_id(0)
    half = y0.shape[0]

    @pl.when(i == 0)
    def _():
        hi, lo = hi_ref[...], lo_ref[...]
        m_ref[:NB] = solve(ta[...], hi, lo)
        m_ref[NB:] = solve(tb[...], hi, lo)

    @pl.when(i < 2)
    def _():
        w_ref[...] = s_ref[i]

    @pl.when(i == 2)
    def _():
        hi, lo = hi_ref[...], lo_ref[...]
        w_ref[:half] = solve(y0[...], hi, lo)
        w_ref[half:] = solve(y1[...], hi, lo)

    @pl.when(i == 3)
    def _():
        hi, lo = hi_ref[...], lo_ref[...]
        w_ref[:half] = solve(ky0[...], hi, lo)
        w_ref[half:] = solve(ky1[...], hi, lo)

    update = lax.dot_general(
        w_ref[...], m_ref[...], (((1,), (1,)), ((), ())), preferred_element_type=F32
    )
    o_ref[...] = (t_ref[...].astype(F32) - update).astype(BF16)


def final(c, trailing, s, rest, ta, tb, hi, lo):
    rows, cols = trailing.shape
    n = rows // 4
    vmem = pl.BlockSpec(memory_space=pltpu.VMEM)
    block = pl.BlockSpec((n, cols), lambda i, c_ref: (c_ref[0] ^ i, 0))
    return pl.pallas_call(
        final_kernel,
        out_shape=jax.ShapeDtypeStruct((rows, cols), BF16),
        grid_spec=pltpu.PrefetchScalarGridSpec(
            num_scalar_prefetch=1,
            grid=(4,),
            in_specs=[block] + [vmem] * 9,
            out_specs=block,
            scratch_shapes=[
                pltpu.VMEM((2 * NB, NB), BF16),
                pltpu.VMEM((n, NB), BF16),
            ],
        ),
        compiler_params=pltpu.CompilerParams(vmem_limit_bytes=24 * 1024 * 1024),
    )(c, trailing, s, *rest, ta, tb, hi, lo)


def widen(value):
    return value.astype(F32) * (1.0 / SCALE)


def local_8x4(trailing, panel, diag_inverse):
    row, col = lax.axis_index("row"), lax.axis_index("col")
    z, x, y, k = row // 2, row % 2, col // 2, col % 2
    barrier = lax.optimization_barrier
    c = jnp.full((1,), col, jnp.int32)
    inv = diag_inverse.T
    n = panel.shape[0]

    mate = send(panel, CORE)
    inv_y = send(inv, ACROSS)
    p0 = (panel[:NB] * SCALE).astype(F16)
    p1 = (panel[NB:] * SCALE).astype(F16)
    y0 = send(p0, ACROSS)
    top = (jnp.where(k == 0, panel[:NB], mate[:NB]) * SCALE).astype(F16)
    r1, r2, r3 = (send(top, spread(j)) for j in (1, 2, 3))
    y1 = send(p1, ACROSS)
    y0, r1 = barrier((y0, r1))
    ky0 = send(y0, CORE)
    across_top = jnp.where(k == 0, y0, ky0)
    same = z % 2 == y
    q0 = jnp.where(same, jnp.where(y == 0, top, across_top), r1)
    q1 = jnp.where(same, r2, r3)
    x0, x1 = send(q0, ASIDE), send(q1, ASIDE)
    inv_k = send(inv, CORE)
    inv_ky = send(inv_y, CORE)
    s, hi, lo = early(c, panel, mate, (inv, inv_k, inv_y, inv_ky))
    ky1 = send(y1, CORE)
    here = x == k
    a = jnp.where(here, q0, x0)
    b = jnp.where(here, q1, x1)
    ta = widen(jnp.where(z < 2, a, b))
    tb = widen(jnp.where(z < 2, b, a))
    rest = [widen(v) for v in (y0, y1, ky0, ky1)]
    return final(c, trailing, s, rest, ta, tb, hi, lo)


def solution(mesh):
    in_specs = (P("row", "col"), P(("row", "col"), None), P(None, "col"))
    out_specs = P("row", "col")
    fits = mesh.shape["row"] == 8 and mesh.shape["col"] == 4
    return jax.shard_map(
        local_8x4 if fits else local_any,
        mesh=mesh,
        in_specs=in_specs,
        out_specs=out_specs,
        check_vma=False,
    )
```

```python
import jax
import jax.numpy as jnp
from jax import lax
from jax.experimental import pallas as pl
from jax.experimental.pallas import tpu as pltpu
from jax.sharding import PartitionSpec as P

NB = 256
SBLK = 2
SCALE = 32768.0
AXES = ("row", "col")
F32, F16, BF16 = jnp.float32, jnp.float16, jnp.bfloat16


def from_root(value, axis, source):
    kept = jnp.where(lax.axis_index(axis) == source, value, 0).astype(value.dtype)
    return lax.psum(kept, axis)


def solve_rows(rows_in, inverse):
    return lax.dot_general(
        rows_in,
        inverse,
        (((1,), (1,)), ((), ())),
        precision=lax.Precision.HIGHEST,
        preferred_element_type=F32,
    ).astype(BF16)


def local_any(trailing, panel, diag_inverse):
    inverse = lax.all_gather(diag_inverse, "col", axis=1, tiled=True)
    raw_rows = lax.all_gather(panel, "col", axis=0, tiled=True)
    solved = solve_rows(raw_rows, inverse)
    top_block = solved[:NB]
    col_index = lax.axis_index("col")
    col_count = lax.axis_size("col")
    pieces = []
    for section in range(SBLK):
        pieces.append(from_root(top_block, "row", col_index + section * col_count))
    mirror = jnp.concatenate(pieces, 0)
    update = lax.dot_general(
        solved, mirror, (((1,), (1,)), ((), ())), preferred_element_type=F32
    )
    return (trailing.astype(F32) - update).astype(BF16)


def dev(z, x, y, k):
    return (z * 2 + x) * 4 + y * 2 + k


ALL = [(z, x, y, k) for z in range(4) for x in range(2) for y in range(2) for k in range(2)]
CORE = [(dev(z, x, y, k), dev(z, x, y, 1 - k)) for z, x, y, k in ALL]
ACROSS = [(dev(z, x, y, k), dev(z, x, 1 - y, k)) for z, x, y, k in ALL]


def spread_a():
    pairs = []
    for z in range(4):
        for x in range(2):
            pairs.append((dev(z, x, 0, x), dev(z ^ 1, x, z % 2, x)))
            pairs.append((dev(z, x, 0, 1 - x), dev(z ^ 2, x, z % 2, x)))
            pairs.append((dev(z, x, 1, x), dev(z, x, 1, 1 - x)))
            pairs.append((dev(z, x, 1, 1 - x), dev(z, x, 0, 1 - x)))
    return pairs


def spread_b():
    pairs = []
    for z in range(4):
        for x in range(2):
            pairs.append((dev(z, x, 0, x), dev(z ^ 3, x, z % 2, x)))
            if z % 2:
                pairs.append((dev(z, x, 0, 1 - x), dev(z, x, 1, x)))
                pairs.append((dev(z, x, 1, x), dev(z, x, 1, 1 - x)))
                pairs.append((dev(z, x, 1, 1 - x), dev(z, x, 0, 1 - x)))
            else:
                pairs.append((dev(z, x, 0, 1 - x), dev(z, x, 0, x)))
                pairs.append((dev(z, x, 1, x), dev(z, x, 1, 1 - x)))
                pairs.append((dev(z, x, 1, 1 - x), dev(z, x, 0, 1 - x)))
    return pairs


ASIDE = [
    (dev(z, x, y, k), dev(z, 1 - x, y, k) if k == x else dev(z, x, y, 1 - k))
    for z, x, y, k in ALL
]


def send(value, pairs):
    return lax.ppermute(value, AXES, pairs)


def split(value):
    high = value.astype(BF16)
    return high, (value - high.astype(F32)).astype(BF16)


def mul(a, b):
    return jnp.dot(a, b, preferred_element_type=F32)


def solve(rows, lt_hi, lt_lo):
    hi, lo = split(rows)
    return (mul(hi, lt_hi) + (mul(hi, lt_lo) + mul(lo, lt_hi))).astype(BF16)


def early_kernel(c_ref, own_ref, mate_ref, l0, l1, l2, l3, s_ref, hi_ref, lo_ref, lt_ref):
    c = c_ref[0]
    for i, block in enumerate((l0, l1, l2, l3)):
        at = pl.multiple_of((c ^ i) * 64, 64)
        lt_ref[pl.ds(at, 64), :] = block[...]
    hi, lo = split(lt_ref[...])
    hi_ref[...] = hi
    lo_ref[...] = lo
    s_ref[0] = solve(own_ref[...], hi, lo)
    s_ref[1] = solve(mate_ref[...], hi, lo)


VMEM = pl.BlockSpec(memory_space=pltpu.VMEM)
SMEM = pl.BlockSpec(memory_space=pltpu.SMEM)
LIMIT = pltpu.CompilerParams(vmem_limit_bytes=24 * 1024 * 1024)


def early(c, own, mate, blocks):
    n = own.shape[0]
    return pl.pallas_call(
        early_kernel,
        out_shape=(
            jax.ShapeDtypeStruct((2, n, NB), BF16),
            jax.ShapeDtypeStruct((NB, NB), BF16),
            jax.ShapeDtypeStruct((NB, NB), BF16),
        ),
        in_specs=[SMEM] + [VMEM] * 6,
        out_specs=(VMEM, VMEM, VMEM),
        scratch_shapes=[pltpu.VMEM((NB, NB), F32)],
        compiler_params=LIMIT,
    )(c, own, mate, *blocks)


def late_kernel(y0, y1, ky0, ky1, hi_ref, lo_ref, s_ref):
    hi, lo = hi_ref[...], lo_ref[...]
    half = y0.shape[0]
    s_ref[0, :half] = solve(y0[...], hi, lo)
    s_ref[0, half:] = solve(y1[...], hi, lo)
    s_ref[1, :half] = solve(ky0[...], hi, lo)
    s_ref[1, half:] = solve(ky1[...], hi, lo)


def late(rest, hi, lo):
    return pl.pallas_call(
        late_kernel,
        out_shape=jax.ShapeDtypeStruct((2, 2 * rest[0].shape[0], NB), BF16),
        in_specs=[VMEM] * 6,
        out_specs=VMEM,
        compiler_params=LIMIT,
    )(*rest, hi, lo)


def final_kernel(c_ref, t_ref, sa, sb, ta, tb, hi_ref, lo_ref, o_ref, m_ref, buf, sems):
    c = c_ref[0]
    n = sa.shape[1]
    hi, lo = hi_ref[...], lo_ref[...]
    m_ref[:NB] = solve(ta[...], hi, lo)
    m_ref[NB:] = solve(tb[...], hi, lo)
    mirror = m_ref[...]
    copies = []
    for i in range(4):
        at = pl.multiple_of((c ^ i) * n, n)
        rows = (sa if i < 2 else sb)[i % 2]
        update = lax.dot_general(
            rows, mirror, (((1,), (1,)), ((), ())), preferred_element_type=F32
        )
        buf[i] = (t_ref[pl.ds(at, n), :].astype(F32) - update).astype(BF16)
        copy = pltpu.make_async_copy(buf.at[i], o_ref.at[pl.ds(at, n), :], sems.at[i])
        copy.start()
        copies.append(copy)
    for copy in copies:
        copy.wait()


def final(c, trailing, sa, sb, ta, tb, hi, lo):
    rows, cols = trailing.shape
    n = rows // 4
    return pl.pallas_call(
        final_kernel,
        out_shape=jax.ShapeDtypeStruct((rows, cols), BF16),
        in_specs=[SMEM] + [VMEM] * 7,
        out_specs=pl.BlockSpec(memory_space=pl.ANY),
        scratch_shapes=[
            pltpu.VMEM((2 * NB, NB), BF16),
            pltpu.VMEM((4, n, cols), BF16),
            pltpu.SemaphoreType.DMA((4,)),
        ],
        compiler_params=LIMIT,
    )(c, trailing, sa, sb, ta, tb, hi, lo)


def widen(value):
    return value.astype(F32) * (1.0 / SCALE)


def narrow(value):
    return (value * SCALE).astype(F16)


def local_8x4(trailing, panel, diag_inverse):
    row, col = lax.axis_index("row"), lax.axis_index("col")
    z, x, y, k = row // 2, row % 2, col // 2, col % 2
    barrier = lax.optimization_barrier
    c = jnp.full((1,), col, jnp.int32)
    inv = diag_inverse.T

    mate = send(panel, CORE)
    inv_y = send(inv, ACROSS)
    y0 = send(narrow(panel[:NB]), ACROSS)
    y1 = send(narrow(panel[NB:]), ACROSS)
    top = narrow(jnp.where(k == 0, panel[:NB], mate[:NB]))
    ra, rb = send(top, spread_a()), send(top, spread_b())
    ky0, ky1 = send(y0, CORE), send(y1, CORE)
    rb = jnp.where((y == 0) & (z % 2 == 0), top, rb)
    r = jnp.concatenate([ra, rb], 0)
    xr = send(r, ASIDE)
    inv_k = send(inv, CORE)
    inv_ky = send(inv_y, CORE)
    sa, hi, lo = early(c, panel, mate, (inv, inv_k, inv_y, inv_ky))
    sb = late([widen(v) for v in (y0, y1, ky0, ky1)], hi, lo)
    here = x == k
    a = jnp.where(here, r[:NB], xr[:NB])
    b = jnp.where(here, r[NB:], xr[NB:])
    a_low = jnp.where(z % 2 == y, z >= 2, z < 2)
    ta = widen(jnp.where(a_low, a, b))
    tb = widen(jnp.where(a_low, b, a))
    return final(c, trailing, sa, sb, ta, tb, hi, lo)


def solution(mesh):
    in_specs = (P("row", "col"), P(("row", "col"), None), P(None, "col"))
    out_specs = P("row", "col")
    fits = mesh.shape["row"] == 8 and mesh.shape["col"] == 4
    return jax.shard_map(
        local_8x4 if fits else local_any,
        mesh=mesh,
        in_specs=in_specs,
        out_specs=out_specs,
        check_vma=False,
    )
```

```python
import jax
import jax.numpy as jnp
from jax import lax
from jax.experimental import pallas as pl
from jax.experimental.pallas import tpu as pltpu
from jax.sharding import PartitionSpec as P

NB = 256
SBLK = 2
SCALE = 32768.0
ORDER = (
    ((0, 0), 0, 0), ((0, 1), 0, 1), ((0, 2), 1, 0), ((0, 3), 1, 1),
    ((1, 0), 2, 0), ((1, 1), 2, 1), ((1, 2), 3, 0), ((1, 3), 3, 1),
)
AXES = ("row", "col")
F32, F16, BF16 = jnp.float32, jnp.float16, jnp.bfloat16


def from_root(value, axis, source):
    kept = jnp.where(lax.axis_index(axis) == source, value, 0).astype(value.dtype)
    return lax.psum(kept, axis)


def solve_rows(rows_in, inverse):
    return lax.dot_general(
        rows_in,
        inverse,
        (((1,), (1,)), ((), ())),
        precision=lax.Precision.HIGHEST,
        preferred_element_type=F32,
    ).astype(BF16)


def local_any(trailing, panel, diag_inverse):
    inverse = lax.all_gather(diag_inverse, "col", axis=1, tiled=True)
    raw_rows = lax.all_gather(panel, "col", axis=0, tiled=True)
    solved = solve_rows(raw_rows, inverse)
    top_block = solved[:NB]
    col_index = lax.axis_index("col")
    col_count = lax.axis_size("col")
    pieces = []
    for section in range(SBLK):
        pieces.append(from_root(top_block, "row", col_index + section * col_count))
    mirror = jnp.concatenate(pieces, 0)
    update = lax.dot_general(
        solved, mirror, (((1,), (1,)), ((), ())), preferred_element_type=F32
    )
    return (trailing.astype(F32) - update).astype(BF16)


def dev(z, x, y, k):
    return (z * 2 + x) * 4 + y * 2 + k


ALL = [(z, x, y, k) for z in range(4) for x in range(2) for y in range(2) for k in range(2)]
CORE = [(dev(z, x, y, k), dev(z, x, y, 1 - k)) for z, x, y, k in ALL]
ACROSS = [(dev(z, x, y, k), dev(z, x, 1 - y, k)) for z, x, y, k in ALL]


def spread_a():
    pairs = []
    for z in range(4):
        for x in range(2):
            pairs.append((dev(z, x, 0, x), dev(z ^ 1, x, z % 2, x)))
            pairs.append((dev(z, x, 0, 1 - x), dev(z ^ 2, x, z % 2, x)))
            pairs.append((dev(z, x, 1, x), dev(z, x, 1, 1 - x)))
            pairs.append((dev(z, x, 1, 1 - x), dev(z, x, 0, 1 - x)))
    return pairs


def spread_b():
    pairs = []
    for z in range(4):
        for x in range(2):
            pairs.append((dev(z, x, 0, x), dev(z ^ 3, x, z % 2, x)))
            if z % 2:
                pairs.append((dev(z, x, 0, 1 - x), dev(z, x, 1, x)))
                pairs.append((dev(z, x, 1, x), dev(z, x, 1, 1 - x)))
                pairs.append((dev(z, x, 1, 1 - x), dev(z, x, 0, 1 - x)))
            else:
                pairs.append((dev(z, x, 0, 1 - x), dev(z, x, 0, x)))
                pairs.append((dev(z, x, 1, x), dev(z, x, 1, 1 - x)))
                pairs.append((dev(z, x, 1, 1 - x), dev(z, x, 0, 1 - x)))
    return pairs


ASIDE = [
    (dev(z, x, y, k), dev(z, 1 - x, y, k) if k == x else dev(z, x, y, 1 - k))
    for z, x, y, k in ALL
]


def send(value, pairs):
    return lax.ppermute(value, AXES, pairs)


def split(value):
    high = value.astype(BF16)
    return high, (value - high.astype(F32)).astype(BF16)


def mul(a, b):
    return jnp.dot(a, b, preferred_element_type=F32)


def solve(rows, lt_hi, lt_lo):
    hi, lo = split(rows)
    return (mul(hi, lt_hi) + (mul(hi, lt_lo) + mul(lo, lt_hi))).astype(BF16)


def early_kernel(c_ref, l0, l1, l2, l3, *refs):
    s_ref, hi_ref, lo_ref, lt_ref = refs[-4:]
    c = c_ref[0]
    for i, block in enumerate((l0, l1, l2, l3)):
        at = pl.multiple_of((c ^ i) * 64, 64)
        lt_ref[pl.ds(at, 64), :] = block[...]
    hi, lo = split(lt_ref[...])
    hi_ref[...] = hi
    lo_ref[...] = lo
    for i, rows in enumerate(refs[:-4]):
        s_ref[2 * i : 2 * i + 2] = solve(rows[...], hi, lo).reshape(2, -1, NB)


VMEM = pl.BlockSpec(memory_space=pltpu.VMEM)
SMEM = pl.BlockSpec(memory_space=pltpu.SMEM)
LIMIT = pltpu.CompilerParams(vmem_limit_bytes=24 * 1024 * 1024)


def early(c, blocks, parts):
    n = parts[0].shape[0]
    return pl.pallas_call(
        early_kernel,
        out_shape=(
            jax.ShapeDtypeStruct((2 * len(parts), n // 2, NB), BF16),
            jax.ShapeDtypeStruct((NB, NB), BF16),
            jax.ShapeDtypeStruct((NB, NB), BF16),
        ),
        in_specs=[SMEM] + [VMEM] * (4 + len(parts)),
        out_specs=(VMEM, VMEM, VMEM),
        scratch_shapes=[pltpu.VMEM((NB, NB), F32)],
        compiler_params=LIMIT,
    )(c, *blocks, *parts)


def late_kernel(hi_ref, lo_ref, *refs):
    hi, lo = hi_ref[...], lo_ref[...]
    for i, rows in enumerate(refs[:-1]):
        refs[-1][2 * i : 2 * i + 2] = solve(rows[...], hi, lo).reshape(2, -1, NB)


def late(hi, lo, parts):
    n = parts[0].shape[0]
    return pl.pallas_call(
        late_kernel,
        out_shape=jax.ShapeDtypeStruct((2 * len(parts), n // 2, NB), BF16),
        in_specs=[VMEM] * (2 + len(parts)),
        out_specs=VMEM,
        compiler_params=LIMIT,
    )(hi, lo, *parts)


def final_kernel(c_ref, t_ref, sa, sb, ta, tb, hi_ref, lo_ref, o_ref, m_ref, buf, sems):
    c = c_ref[0]
    n = buf.shape[1]
    hi, lo = hi_ref[...], lo_ref[...]
    m_ref[:NB] = solve(ta[...], hi, lo)
    m_ref[NB:] = solve(tb[...], hi, lo)
    mirror = m_ref[...]
    copies = []
    for i, (source, part, row) in enumerate(ORDER):
        at = pl.multiple_of((c ^ part) * 2 * n + row * n, n)
        rows = (sa, sb)[source[0]][source[1]]
        update = lax.dot_general(
            rows, mirror, (((1,), (1,)), ((), ())), preferred_element_type=F32
        )
        buf[i] = (t_ref[pl.ds(at, n), :].astype(F32) - update).astype(BF16)
        copy = pltpu.make_async_copy(buf.at[i], o_ref.at[pl.ds(at, n), :], sems.at[i])
        copy.start()
        copies.append(copy)
    for copy in copies:
        copy.wait()


def final(c, trailing, sa, sb, ta, tb, hi, lo):
    rows, cols = trailing.shape
    n = rows // 8
    return pl.pallas_call(
        final_kernel,
        out_shape=jax.ShapeDtypeStruct((rows, cols), BF16),
        in_specs=[SMEM] + [VMEM] * 7,
        out_specs=pl.BlockSpec(memory_space=pl.ANY),
        scratch_shapes=[
            pltpu.VMEM((2 * NB, NB), BF16),
            pltpu.VMEM((8, n, cols), BF16),
            pltpu.SemaphoreType.DMA((8,)),
        ],
        compiler_params=LIMIT,
    )(c, trailing, sa, sb, ta, tb, hi, lo)


def widen(value):
    return value.astype(F32) * (1.0 / SCALE)


def narrow(value):
    return (value * SCALE).astype(F16)


def local_8x4(trailing, panel, diag_inverse):
    row, col = lax.axis_index("row"), lax.axis_index("col")
    z, x, y, k = row // 2, row % 2, col // 2, col % 2
    barrier = lax.optimization_barrier
    c = jnp.full((1,), col, jnp.int32)
    inv = diag_inverse.T

    mate = send(panel, CORE)
    inv_y = send(inv, ACROSS)
    p, m = narrow(panel), narrow(mate)
    top = jnp.where(k == 0, p[:NB], m[:NB])
    p, m, top = barrier((p, m, top))
    yp = send(p, ACROSS)
    ra, rb = send(top, spread_a()), send(top, spread_b())
    ra, rb, inv, inv_y = barrier((ra, rb, inv, inv_y))
    inv_k = send(inv, CORE)
    inv_ky = send(inv_y, CORE)
    r = jnp.concatenate([ra, rb], 0)
    xr = send(r, ASIDE)
    kyp = send(yp, CORE)
    blocks = (inv, inv_k, inv_y, inv_ky)
    sa, hi, lo = early(c, blocks, [widen(v) for v in (p, m)])
    sb = late(hi, lo, [widen(v) for v in (yp, kyp)])
    here = x == k
    a = jnp.where(here, r[:NB], xr[:NB])
    b = jnp.where(here, r[NB:], xr[NB:])
    a_low = jnp.where(z % 2 == y, z >= 2, z < 2)
    ta = widen(jnp.where(a_low, a, b))
    tb = widen(jnp.where(a_low, b, a))
    return final(c, trailing, sa, sb, ta, tb, hi, lo)


def solution(mesh):
    in_specs = (P("row", "col"), P(("row", "col"), None), P(None, "col"))
    out_specs = P("row", "col")
    fits = mesh.shape["row"] == 8 and mesh.shape["col"] == 4
    return jax.shard_map(
        local_8x4 if fits else local_any,
        mesh=mesh,
        in_specs=in_specs,
        out_specs=out_specs,
        check_vma=False,
    )
```

```python
import jax
import jax.numpy as jnp
from jax import lax
from jax.experimental import pallas as pl
from jax.experimental.pallas import tpu as pltpu
from jax.sharding import PartitionSpec as P

NB = 256
SBLK = 2
SCALE = 32768.0
ORDER = (
    ((0, 0), 0, 0), ((0, 1), 0, 1), ((0, 2), 1, 0), ((0, 3), 1, 1),
    ((1, 0), 2, 0), ((1, 1), 2, 1), ((1, 2), 3, 0), ((1, 3), 3, 1),
)
AXES = ("row", "col")
F32, F16, BF16 = jnp.float32, jnp.float16, jnp.bfloat16


def from_root(value, axis, source):
    kept = jnp.where(lax.axis_index(axis) == source, value, 0).astype(value.dtype)
    return lax.psum(kept, axis)


def solve_rows(rows_in, inverse):
    return lax.dot_general(
        rows_in,
        inverse,
        (((1,), (1,)), ((), ())),
        precision=lax.Precision.HIGHEST,
        preferred_element_type=F32,
    ).astype(BF16)


def local_any(trailing, panel, diag_inverse):
    inverse = lax.all_gather(diag_inverse, "col", axis=1, tiled=True)
    raw_rows = lax.all_gather(panel, "col", axis=0, tiled=True)
    solved = solve_rows(raw_rows, inverse)
    top_block = solved[:NB]
    col_index = lax.axis_index("col")
    col_count = lax.axis_size("col")
    pieces = []
    for section in range(SBLK):
        pieces.append(from_root(top_block, "row", col_index + section * col_count))
    mirror = jnp.concatenate(pieces, 0)
    update = lax.dot_general(
        solved, mirror, (((1,), (1,)), ((), ())), preferred_element_type=F32
    )
    return (trailing.astype(F32) - update).astype(BF16)


def dev(z, x, y, k):
    return (z * 2 + x) * 4 + y * 2 + k


ALL = [(z, x, y, k) for z in range(4) for x in range(2) for y in range(2) for k in range(2)]
CORE = [(dev(z, x, y, k), dev(z, x, y, 1 - k)) for z, x, y, k in ALL]
ACROSS = [(dev(z, x, y, k), dev(z, x, 1 - y, k)) for z, x, y, k in ALL]


def spread_a():
    pairs = []
    for z in range(4):
        for x in range(2):
            pairs.append((dev(z, x, 0, x), dev(z ^ 1, x, z % 2, x)))
            pairs.append((dev(z, x, 0, 1 - x), dev(z ^ 2, x, z % 2, x)))
            pairs.append((dev(z, x, 1, x), dev(z, x, 1, 1 - x)))
            pairs.append((dev(z, x, 1, 1 - x), dev(z, x, 0, 1 - x)))
    return pairs


def spread_b():
    pairs = []
    for z in range(4):
        for x in range(2):
            pairs.append((dev(z, x, 0, x), dev(z ^ 3, x, z % 2, x)))
            if z % 2:
                pairs.append((dev(z, x, 0, 1 - x), dev(z, x, 1, x)))
                pairs.append((dev(z, x, 1, x), dev(z, x, 1, 1 - x)))
                pairs.append((dev(z, x, 1, 1 - x), dev(z, x, 0, 1 - x)))
            else:
                pairs.append((dev(z, x, 0, 1 - x), dev(z, x, 0, x)))
                pairs.append((dev(z, x, 1, x), dev(z, x, 1, 1 - x)))
                pairs.append((dev(z, x, 1, 1 - x), dev(z, x, 0, 1 - x)))
    return pairs


ASIDE = [
    (dev(z, x, y, k), dev(z, 1 - x, y, k) if k == x else dev(z, x, y, 1 - k))
    for z, x, y, k in ALL
]


def send(value, pairs):
    return lax.ppermute(value, AXES, pairs)


def split(value):
    high = value.astype(BF16)
    return high, (value - high.astype(F32)).astype(BF16)


def mul(a, b):
    return jnp.dot(a, b, preferred_element_type=F32)


def solve(rows, lt_hi, lt_lo):
    hi, lo = split(rows)
    return (mul(hi, lt_hi) + (mul(hi, lt_lo) + mul(lo, lt_hi))).astype(BF16)


def early_kernel(c_ref, l0, l1, l2, l3, *refs):
    s_ref, hi_ref, lo_ref, lt_ref = refs[-4:]
    c = c_ref[0]
    for i, block in enumerate((l0, l1, l2, l3)):
        at = pl.multiple_of((c ^ i) * 64, 64)
        lt_ref[pl.ds(at, 64), :] = block[...]
    hi, lo = split(lt_ref[...])
    hi_ref[...] = hi
    lo_ref[...] = lo
    for i, rows in enumerate(refs[:-4]):
        s_ref[i] = solve(rows[...], hi, lo)


VMEM = pl.BlockSpec(memory_space=pltpu.VMEM)
SMEM = pl.BlockSpec(memory_space=pltpu.SMEM)
LIMIT = pltpu.CompilerParams(vmem_limit_bytes=24 * 1024 * 1024)


def early(c, blocks, parts):
    n = parts[0].shape[0]
    return pl.pallas_call(
        early_kernel,
        out_shape=(
            jax.ShapeDtypeStruct((len(parts), n, NB), BF16),
            jax.ShapeDtypeStruct((NB, NB), BF16),
            jax.ShapeDtypeStruct((NB, NB), BF16),
        ),
        in_specs=[SMEM] + [VMEM] * (4 + len(parts)),
        out_specs=(VMEM, VMEM, VMEM),
        scratch_shapes=[pltpu.VMEM((NB, NB), F32)],
        compiler_params=LIMIT,
    )(c, *blocks, *parts)


def late_kernel(hi_ref, lo_ref, *refs):
    hi, lo = hi_ref[...], lo_ref[...]
    for i, rows in enumerate(refs[:-1]):
        refs[-1][i] = solve(rows[...], hi, lo)


def late(hi, lo, parts):
    n = parts[0].shape[0]
    return pl.pallas_call(
        late_kernel,
        out_shape=jax.ShapeDtypeStruct((len(parts), n, NB), BF16),
        in_specs=[VMEM] * (2 + len(parts)),
        out_specs=VMEM,
        compiler_params=LIMIT,
    )(hi, lo, *parts)


def final_kernel(c_ref, t_ref, sa, sb, ta, tb, hi_ref, lo_ref, o_ref, m_ref, buf, sems):
    c = c_ref[0]
    n = buf.shape[1]
    hi, lo = hi_ref[...], lo_ref[...]
    m_ref[:NB] = solve(ta[...], hi, lo)
    m_ref[NB:] = solve(tb[...], hi, lo)
    mirror = m_ref[...]
    copies = []
    for i, (source, part, row) in enumerate(ORDER):
        at = pl.multiple_of((c ^ part) * 2 * n + row * n, n)
        rows = (sa, sb)[source[0]][source[1]]
        update = lax.dot_general(
            rows, mirror, (((1,), (1,)), ((), ())), preferred_element_type=F32
        )
        buf[i] = (t_ref[pl.ds(at, n), :].astype(F32) - update).astype(BF16)
        copy = pltpu.make_async_copy(buf.at[i], o_ref.at[pl.ds(at, n), :], sems.at[i])
        copy.start()
        copies.append(copy)
    for copy in copies:
        copy.wait()


def final(c, trailing, sa, sb, ta, tb, hi, lo):
    rows, cols = trailing.shape
    n = rows // 8
    return pl.pallas_call(
        final_kernel,
        out_shape=jax.ShapeDtypeStruct((rows, cols), BF16),
        in_specs=[SMEM] + [VMEM] * 7,
        out_specs=pl.BlockSpec(memory_space=pl.ANY),
        scratch_shapes=[
            pltpu.VMEM((2 * NB, NB), BF16),
            pltpu.VMEM((8, n, cols), BF16),
            pltpu.SemaphoreType.DMA((8,)),
        ],
        compiler_params=LIMIT,
    )(c, trailing, sa, sb, ta, tb, hi, lo)


def widen(value):
    return value.astype(F32) * (1.0 / SCALE)


def narrow(value):
    return (value * SCALE).astype(F16)


def local_8x4(trailing, panel, diag_inverse):
    row, col = lax.axis_index("row"), lax.axis_index("col")
    z, x, y, k = row // 2, row % 2, col // 2, col % 2
    barrier = lax.optimization_barrier
    c = jnp.full((1,), col, jnp.int32)
    inv = diag_inverse.T

    mate = send(panel, CORE)
    inv_y = send(inv, ACROSS)
    p, m = narrow(panel), narrow(mate)
    top = jnp.where(k == 0, p[:NB], m[:NB])
    p, m, top = barrier((p, m, top))
    y0, y1 = send(p[:NB], ACROSS), send(p[NB:], ACROSS)
    ra, rb = send(top, spread_a()), send(top, spread_b())
    r = jnp.concatenate([ra, rb], 0)
    xr = send(r, ASIDE)
    inv_y, inv, *_ = barrier((inv_y, inv, r))
    y0, y1, *_ = barrier((y0, y1, r))
    inv_k, inv_ky = send(inv, CORE), send(inv_y, CORE)
    ky0, ky1 = send(y0, CORE), send(y1, CORE)
    blocks = (inv, inv_k, inv_y, inv_ky)
    s, hi, lo = early(c, blocks, [widen(v) for v in (p[:NB], p[NB:], m[:NB], m[NB:])])
    sb = late(hi, lo, [widen(v) for v in (y0, y1, ky0, ky1)])
    sa = s
    here = x == k
    a = jnp.where(here, r[:NB], xr[:NB])
    b = jnp.where(here, r[NB:], xr[NB:])
    a_low = jnp.where(z % 2 == y, z >= 2, z < 2)
    ta = widen(jnp.where(a_low, a, b))
    tb = widen(jnp.where(a_low, b, a))
    return final(c, trailing, sa, sb, ta, tb, hi, lo)


def solution(mesh):
    in_specs = (P("row", "col"), P(("row", "col"), None), P(None, "col"))
    out_specs = P("row", "col")
    fits = mesh.shape["row"] == 8 and mesh.shape["col"] == 4
    return jax.shard_map(
        local_8x4 if fits else local_any,
        mesh=mesh,
        in_specs=in_specs,
        out_specs=out_specs,
        check_vma=False,
    )
```

```python
import jax
import jax.numpy as jnp
from jax import lax
from jax.experimental import pallas as pl
from jax.experimental.pallas import tpu as pltpu
from jax.sharding import PartitionSpec as P

NB = 256
SBLK = 2
SCALE = 32768.0
ORDER = (
    ((0, 0), 0, 0), ((0, 1), 0, 1), ((0, 2), 1, 0), ((0, 3), 1, 1),
    ((1, 0), 2, 0), ((1, 1), 2, 1), ((1, 2), 3, 0), ((1, 3), 3, 1),
)
AXES = ("row", "col")
F32, F16, BF16 = jnp.float32, jnp.float16, jnp.bfloat16


def from_root(value, axis, source):
    kept = jnp.where(lax.axis_index(axis) == source, value, 0).astype(value.dtype)
    return lax.psum(kept, axis)


def solve_rows(rows_in, inverse):
    return lax.dot_general(
        rows_in,
        inverse,
        (((1,), (1,)), ((), ())),
        precision=lax.Precision.HIGHEST,
        preferred_element_type=F32,
    ).astype(BF16)


def local_any(trailing, panel, diag_inverse):
    inverse = lax.all_gather(diag_inverse, "col", axis=1, tiled=True)
    raw_rows = lax.all_gather(panel, "col", axis=0, tiled=True)
    solved = solve_rows(raw_rows, inverse)
    top_block = solved[:NB]
    col_index = lax.axis_index("col")
    col_count = lax.axis_size("col")
    pieces = []
    for section in range(SBLK):
        pieces.append(from_root(top_block, "row", col_index + section * col_count))
    mirror = jnp.concatenate(pieces, 0)
    update = lax.dot_general(
        solved, mirror, (((1,), (1,)), ((), ())), preferred_element_type=F32
    )
    return (trailing.astype(F32) - update).astype(BF16)


def dev(z, x, y, k):
    return (z * 2 + x) * 4 + y * 2 + k


ALL = [(z, x, y, k) for z in range(4) for x in range(2) for y in range(2) for k in range(2)]
CORE = [(dev(z, x, y, k), dev(z, x, y, 1 - k)) for z, x, y, k in ALL]
ACROSS = [(dev(z, x, y, k), dev(z, x, 1 - y, k)) for z, x, y, k in ALL]


def spread_a():
    pairs = []
    for z in range(4):
        for x in range(2):
            pairs.append((dev(z, x, 0, x), dev(z ^ 1, x, z % 2, x)))
            pairs.append((dev(z, x, 0, 1 - x), dev(z ^ 2, x, z % 2, x)))
            pairs.append((dev(z, x, 1, x), dev(z, x, 1, 1 - x)))
            pairs.append((dev(z, x, 1, 1 - x), dev(z, x, 0, 1 - x)))
    return pairs


def spread_b():
    pairs = []
    for z in range(4):
        for x in range(2):
            pairs.append((dev(z, x, 0, x), dev(z ^ 3, x, z % 2, x)))
            if z % 2:
                pairs.append((dev(z, x, 0, 1 - x), dev(z, x, 1, x)))
                pairs.append((dev(z, x, 1, x), dev(z, x, 1, 1 - x)))
                pairs.append((dev(z, x, 1, 1 - x), dev(z, x, 0, 1 - x)))
            else:
                pairs.append((dev(z, x, 0, 1 - x), dev(z, x, 0, x)))
                pairs.append((dev(z, x, 1, x), dev(z, x, 1, 1 - x)))
                pairs.append((dev(z, x, 1, 1 - x), dev(z, x, 0, 1 - x)))
    return pairs


ASIDE = [
    (dev(z, x, y, k), dev(z, 1 - x, y, k) if k == x else dev(z, x, y, 1 - k))
    for z, x, y, k in ALL
]


def send(value, pairs):
    return lax.ppermute(value, AXES, pairs)


def split(value):
    high = value.astype(BF16)
    return high, (value - high.astype(F32)).astype(BF16)


def mul(a, b):
    return jnp.dot(a, b, preferred_element_type=F32)


def solve(rows, lt_hi, lt_lo):
    hi, lo = split(rows)
    return (mul(hi, lt_hi) + (mul(hi, lt_lo) + mul(lo, lt_hi))).astype(BF16)


def early_kernel(c_ref, l0, l1, l2, l3, *refs):
    s_ref, hi_ref, lo_ref, lt_ref = refs[-4:]
    c = c_ref[0]
    for i, block in enumerate((l0, l1, l2, l3)):
        at = pl.multiple_of((c ^ i) * 64, 64)
        lt_ref[pl.ds(at, 64), :] = block[...]
    hi, lo = split(lt_ref[...])
    hi_ref[...] = hi
    lo_ref[...] = lo
    for i, rows in enumerate(refs[:-4]):
        s_ref[i] = solve(rows[...], hi, lo)


VMEM = pl.BlockSpec(memory_space=pltpu.VMEM)
SMEM = pl.BlockSpec(memory_space=pltpu.SMEM)
LIMIT = pltpu.CompilerParams(vmem_limit_bytes=24 * 1024 * 1024)


def early(c, blocks, parts):
    n = parts[0].shape[0]
    return pl.pallas_call(
        early_kernel,
        out_shape=(
            jax.ShapeDtypeStruct((len(parts), n, NB), BF16),
            jax.ShapeDtypeStruct((NB, NB), BF16),
            jax.ShapeDtypeStruct((NB, NB), BF16),
        ),
        in_specs=[SMEM] + [VMEM] * (4 + len(parts)),
        out_specs=(VMEM, VMEM, VMEM),
        scratch_shapes=[pltpu.VMEM((NB, NB), F32)],
        compiler_params=LIMIT,
    )(c, *blocks, *parts)


def late_kernel(hi_ref, lo_ref, *refs):
    hi, lo = hi_ref[...], lo_ref[...]
    for i, rows in enumerate(refs[:-1]):
        refs[-1][i] = solve(rows[...], hi, lo)


def late(hi, lo, parts):
    n = parts[0].shape[0]
    return pl.pallas_call(
        late_kernel,
        out_shape=jax.ShapeDtypeStruct((len(parts), n, NB), BF16),
        in_specs=[VMEM] * (2 + len(parts)),
        out_specs=VMEM,
        compiler_params=LIMIT,
    )(hi, lo, *parts)


def final_kernel(c_ref, t_ref, sa, sb, ta, tb, hi_ref, lo_ref, o_ref, m_ref, buf, sems):
    c = c_ref[0]
    n = buf.shape[1]
    hi, lo = hi_ref[...], lo_ref[...]
    m_ref[:NB] = solve(ta[...], hi, lo)
    m_ref[NB:] = solve(tb[...], hi, lo)
    mirror = m_ref[...]
    copies = []
    for i, (source, part, row) in enumerate(ORDER):
        at = pl.multiple_of((c ^ part) * 2 * n + row * n, n)
        rows = (sa, sb)[source[0]][source[1]]
        update = lax.dot_general(
            rows, mirror, (((1,), (1,)), ((), ())), preferred_element_type=F32
        )
        buf[i] = (t_ref[pl.ds(at, n), :].astype(F32) - update).astype(BF16)
        copy = pltpu.make_async_copy(buf.at[i], o_ref.at[pl.ds(at, n), :], sems.at[i])
        copy.start()
        copies.append(copy)
    for copy in copies:
        copy.wait()


def final(c, trailing, sa, sb, ta, tb, hi, lo):
    rows, cols = trailing.shape
    n = rows // 8
    return pl.pallas_call(
        final_kernel,
        out_shape=jax.ShapeDtypeStruct((rows, cols), BF16),
        in_specs=[SMEM] + [VMEM] * 7,
        out_specs=pl.BlockSpec(memory_space=pl.ANY),
        scratch_shapes=[
            pltpu.VMEM((2 * NB, NB), BF16),
            pltpu.VMEM((8, n, cols), BF16),
            pltpu.SemaphoreType.DMA((8,)),
        ],
        compiler_params=LIMIT,
    )(c, trailing, sa, sb, ta, tb, hi, lo)


def widen(value):
    return value.astype(F32) * (1.0 / SCALE)


def narrow(value):
    return (value * SCALE).astype(F16)


def local_8x4(trailing, panel, diag_inverse):
    row, col = lax.axis_index("row"), lax.axis_index("col")
    z, x, y, k = row // 2, row % 2, col // 2, col % 2
    barrier = lax.optimization_barrier
    c = jnp.full((1,), col, jnp.int32)
    inv = diag_inverse.T

    mate = send(panel, CORE)
    inv_y = send(inv, ACROSS)
    p, m = narrow(panel), narrow(mate)
    top = jnp.where(k == 0, p[:NB], m[:NB])
    p, m, top = barrier((p, m, top))
    y0, y1 = send(p[:NB], ACROSS), send(p[NB:], ACROSS)
    ra, rb = send(top, spread_a()), send(top, spread_b())
    r = jnp.concatenate([ra, rb], 0)
    xr = send(r, ASIDE)
    inv_y, inv, *_ = barrier((inv_y, inv, r))
    y1, *_ = barrier((y1, r))
    inv_k, inv_ky = send(inv, CORE), send(inv_y, CORE)
    ky0, ky1 = send(y0, CORE), send(y1, CORE)
    blocks = (inv, inv_k, inv_y, inv_ky)
    s, hi, lo = early(c, blocks, [widen(v) for v in (p[:NB], p[NB:], m[:NB], m[NB:])])
    sb = late(hi, lo, [widen(v) for v in (y0, y1, ky0, ky1)])
    xr, _ = barrier((xr, sb))
    sa = s
    here = x == k
    a = jnp.where(here, r[:NB], xr[:NB])
    b = jnp.where(here, r[NB:], xr[NB:])
    a_low = jnp.where(z % 2 == y, z >= 2, z < 2)
    ta = widen(jnp.where(a_low, a, b))
    tb = widen(jnp.where(a_low, b, a))
    return final(c, trailing, sa, sb, ta, tb, hi, lo)


def solution(mesh):
    in_specs = (P("row", "col"), P(("row", "col"), None), P(None, "col"))
    out_specs = P("row", "col")
    fits = mesh.shape["row"] == 8 and mesh.shape["col"] == 4
    return jax.shard_map(
        local_8x4 if fits else local_any,
        mesh=mesh,
        in_specs=in_specs,
        out_specs=out_specs,
        check_vma=False,
    )
```

```python
import jax
import jax.numpy as jnp
from jax import lax
from jax.experimental import pallas as pl
from jax.experimental.pallas import tpu as pltpu
from jax.sharding import PartitionSpec as P

NB = 256
SBLK = 2
SCALE = 32768.0
ORDER = (
    ((0, 0), 0, 0), ((0, 1), 0, 1), ((0, 2), 1, 0), ((0, 3), 1, 1),
    ((1, 0), 2, 0), ((1, 1), 2, 1), ((1, 2), 3, 0), ((1, 3), 3, 1),
)
AXES = ("row", "col")
F32, F16, BF16 = jnp.float32, jnp.float16, jnp.bfloat16


def from_root(value, axis, source):
    kept = jnp.where(lax.axis_index(axis) == source, value, 0).astype(value.dtype)
    return lax.psum(kept, axis)


def solve_rows(rows_in, inverse):
    return lax.dot_general(
        rows_in,
        inverse,
        (((1,), (1,)), ((), ())),
        precision=lax.Precision.HIGHEST,
        preferred_element_type=F32,
    ).astype(BF16)


def local_any(trailing, panel, diag_inverse):
    inverse = lax.all_gather(diag_inverse, "col", axis=1, tiled=True)
    raw_rows = lax.all_gather(panel, "col", axis=0, tiled=True)
    solved = solve_rows(raw_rows, inverse)
    top_block = solved[:NB]
    col_index = lax.axis_index("col")
    col_count = lax.axis_size("col")
    pieces = []
    for section in range(SBLK):
        pieces.append(from_root(top_block, "row", col_index + section * col_count))
    mirror = jnp.concatenate(pieces, 0)
    update = lax.dot_general(
        solved, mirror, (((1,), (1,)), ((), ())), preferred_element_type=F32
    )
    return (trailing.astype(F32) - update).astype(BF16)


def dev(z, x, y, k):
    return (z * 2 + x) * 4 + y * 2 + k


ALL = [(z, x, y, k) for z in range(4) for x in range(2) for y in range(2) for k in range(2)]
CORE = [(dev(z, x, y, k), dev(z, x, y, 1 - k)) for z, x, y, k in ALL]
ACROSS = [(dev(z, x, y, k), dev(z, x, 1 - y, k)) for z, x, y, k in ALL]


def spread_a():
    pairs = []
    for z in range(4):
        for x in range(2):
            pairs.append((dev(z, x, 0, x), dev(z ^ 1, x, z % 2, x)))
            pairs.append((dev(z, x, 0, 1 - x), dev(z ^ 2, x, z % 2, x)))
            pairs.append((dev(z, x, 1, x), dev(z, x, 1, 1 - x)))
            pairs.append((dev(z, x, 1, 1 - x), dev(z, x, 0, 1 - x)))
    return pairs


def spread_b():
    pairs = []
    for z in range(4):
        for x in range(2):
            pairs.append((dev(z, x, 0, x), dev(z ^ 3, x, z % 2, x)))
            if z % 2:
                pairs.append((dev(z, x, 0, 1 - x), dev(z, x, 1, x)))
                pairs.append((dev(z, x, 1, x), dev(z, x, 1, 1 - x)))
                pairs.append((dev(z, x, 1, 1 - x), dev(z, x, 0, 1 - x)))
            else:
                pairs.append((dev(z, x, 0, 1 - x), dev(z, x, 0, x)))
                pairs.append((dev(z, x, 1, x), dev(z, x, 1, 1 - x)))
                pairs.append((dev(z, x, 1, 1 - x), dev(z, x, 0, 1 - x)))
    return pairs


ASIDE = [
    (dev(z, x, y, k), dev(z, 1 - x, y, k) if k == x else dev(z, x, y, 1 - k))
    for z, x, y, k in ALL
]


def send(value, pairs):
    return lax.ppermute(value, AXES, pairs)


def split(value):
    high = value.astype(BF16)
    return high, (value - high.astype(F32)).astype(BF16)


def mul(a, b):
    return jnp.dot(a, b, preferred_element_type=F32)


def solve(rows, lt_hi, lt_lo):
    hi, lo = split(rows)
    return (mul(hi, lt_hi) + (mul(hi, lt_lo) + mul(lo, lt_hi))).astype(BF16)


def early_kernel(c_ref, _, l0, l1, l2, l3, *refs):
    s_ref, hi_ref, lo_ref, lt_ref = refs[-4:]
    c = c_ref[0]
    for i, block in enumerate((l0, l1, l2, l3)):
        at = pl.multiple_of((c ^ i) * 64, 64)
        lt_ref[pl.ds(at, 64), :] = block[...]
    hi, lo = split(lt_ref[...])
    hi_ref[...] = hi
    lo_ref[...] = lo
    for i, rows in enumerate(refs[:-4]):
        s_ref[i] = solve(rows[...], hi, lo)


VMEM = pl.BlockSpec(memory_space=pltpu.VMEM)
SMEM = pl.BlockSpec(memory_space=pltpu.SMEM)
LIMIT = pltpu.CompilerParams(vmem_limit_bytes=24 * 1024 * 1024)


def early(c, trailing, blocks, parts):
    n = parts[0].shape[0]
    return pl.pallas_call(
        early_kernel,
        out_shape=(
            jax.ShapeDtypeStruct((len(parts), n, NB), BF16),
            jax.ShapeDtypeStruct((NB, NB), BF16),
            jax.ShapeDtypeStruct((NB, NB), BF16),
        ),
        in_specs=[SMEM, VMEM] + [VMEM] * (4 + len(parts)),
        out_specs=(VMEM, VMEM, VMEM),
        scratch_shapes=[pltpu.VMEM((NB, NB), F32)],
        compiler_params=LIMIT,
    )(c, trailing, *blocks, *parts)


def late_kernel(hi_ref, lo_ref, *refs):
    hi, lo = hi_ref[...], lo_ref[...]
    for i, rows in enumerate(refs[:-1]):
        refs[-1][i] = solve(rows[...], hi, lo)


def late(hi, lo, parts):
    n = parts[0].shape[0]
    return pl.pallas_call(
        late_kernel,
        out_shape=jax.ShapeDtypeStruct((len(parts), n, NB), BF16),
        in_specs=[VMEM] * (2 + len(parts)),
        out_specs=VMEM,
        compiler_params=LIMIT,
    )(hi, lo, *parts)


def final_kernel(c_ref, t_ref, sa, sb, ta, tb, hi_ref, lo_ref, o_ref, m_ref, buf, sems):
    c = c_ref[0]
    n = buf.shape[1]
    hi, lo = hi_ref[...], lo_ref[...]
    m_ref[:NB] = solve(ta[...], hi, lo)
    m_ref[NB:] = solve(tb[...], hi, lo)
    mirror = m_ref[...]
    copies = []
    for i, (source, part, row) in enumerate(ORDER):
        at = pl.multiple_of((c ^ part) * 2 * n + row * n, n)
        rows = (sa, sb)[source[0]][source[1]]
        update = lax.dot_general(
            rows, mirror, (((1,), (1,)), ((), ())), preferred_element_type=F32
        )
        buf[i] = (t_ref[pl.ds(at, n), :].astype(F32) - update).astype(BF16)
        copy = pltpu.make_async_copy(buf.at[i], o_ref.at[pl.ds(at, n), :], sems.at[i])
        copy.start()
        copies.append(copy)
    for copy in copies:
        copy.wait()


def final(c, trailing, sa, sb, ta, tb, hi, lo):
    rows, cols = trailing.shape
    n = rows // 8
    return pl.pallas_call(
        final_kernel,
        out_shape=jax.ShapeDtypeStruct((rows, cols), BF16),
        in_specs=[SMEM] + [VMEM] * 7,
        out_specs=pl.BlockSpec(memory_space=pl.ANY),
        scratch_shapes=[
            pltpu.VMEM((2 * NB, NB), BF16),
            pltpu.VMEM((8, n, cols), BF16),
            pltpu.SemaphoreType.DMA((8,)),
        ],
        compiler_params=LIMIT,
    )(c, trailing, sa, sb, ta, tb, hi, lo)


def widen(value):
    return value.astype(F32) * (1.0 / SCALE)


def narrow(value):
    return (value * SCALE).astype(F16)


def local_8x4(trailing, panel, diag_inverse):
    row, col = lax.axis_index("row"), lax.axis_index("col")
    z, x, y, k = row // 2, row % 2, col // 2, col % 2
    barrier = lax.optimization_barrier
    c = jnp.full((1,), col, jnp.int32)
    inv = diag_inverse.T

    mate = send(panel, CORE)
    inv_y = send(inv, ACROSS)
    p, m = narrow(panel), narrow(mate)
    top = jnp.where(k == 0, p[:NB], m[:NB])
    p, m, top = barrier((p, m, top))
    y0, y1 = send(p[:NB], ACROSS), send(p[NB:], ACROSS)
    ra, rb = send(top, spread_a()), send(top, spread_b())
    r = jnp.concatenate([ra, rb], 0)
    xr = send(r, ASIDE)
    inv_y, inv, *_ = barrier((inv_y, inv, r))
    y1, *_ = barrier((y1, r))
    inv_k, inv_ky = send(inv, CORE), send(inv_y, CORE)
    ky0, ky1 = send(y0, CORE), send(y1, CORE)
    blocks = (inv, inv_k, inv_y, inv_ky)
    s, hi, lo = early(c, trailing, blocks, [widen(v) for v in (p[:NB], p[NB:], m[:NB], m[NB:])])
    sb = late(hi, lo, [widen(v) for v in (y0, y1, ky0, ky1)])
    xr, _ = barrier((xr, sb))
    sa = s
    here = x == k
    a = jnp.where(here, r[:NB], xr[:NB])
    b = jnp.where(here, r[NB:], xr[NB:])
    a_low = jnp.where(z % 2 == y, z >= 2, z < 2)
    ta = widen(jnp.where(a_low, a, b))
    tb = widen(jnp.where(a_low, b, a))
    return final(c, trailing, sa, sb, ta, tb, hi, lo)


def solution(mesh):
    in_specs = (P("row", "col"), P(("row", "col"), None), P(None, "col"))
    out_specs = P("row", "col")
    fits = mesh.shape["row"] == 8 and mesh.shape["col"] == 4
    return jax.shard_map(
        local_8x4 if fits else local_any,
        mesh=mesh,
        in_specs=in_specs,
        out_specs=out_specs,
        check_vma=False,
    )
```

```python
import jax
import jax.numpy as jnp
from jax import lax
from jax.experimental import pallas as pl
from jax.experimental.pallas import tpu as pltpu
from jax.sharding import PartitionSpec as P

NB = 256
SBLK = 2
SCALE = 32768.0
ORDER = (
    ((0, 0), 0, 0), ((0, 1), 0, 1), ((0, 2), 1, 0), ((0, 3), 1, 1),
    ((1, 0), 2, 0), ((1, 1), 3, 0), ((2, 0), 2, 1), ((2, 1), 3, 1),
)
AXES = ("row", "col")
F32, F16, BF16 = jnp.float32, jnp.float16, jnp.bfloat16


def from_root(value, axis, source):
    kept = jnp.where(lax.axis_index(axis) == source, value, 0).astype(value.dtype)
    return lax.psum(kept, axis)


def solve_rows(rows_in, inverse):
    return lax.dot_general(
        rows_in,
        inverse,
        (((1,), (1,)), ((), ())),
        precision=lax.Precision.HIGHEST,
        preferred_element_type=F32,
    ).astype(BF16)


def local_any(trailing, panel, diag_inverse):
    inverse = lax.all_gather(diag_inverse, "col", axis=1, tiled=True)
    raw_rows = lax.all_gather(panel, "col", axis=0, tiled=True)
    solved = solve_rows(raw_rows, inverse)
    top_block = solved[:NB]
    col_index = lax.axis_index("col")
    col_count = lax.axis_size("col")
    pieces = []
    for section in range(SBLK):
        pieces.append(from_root(top_block, "row", col_index + section * col_count))
    mirror = jnp.concatenate(pieces, 0)
    update = lax.dot_general(
        solved, mirror, (((1,), (1,)), ((), ())), preferred_element_type=F32
    )
    return (trailing.astype(F32) - update).astype(BF16)


def dev(z, x, y, k):
    return (z * 2 + x) * 4 + y * 2 + k


ALL = [(z, x, y, k) for z in range(4) for x in range(2) for y in range(2) for k in range(2)]
CORE = [(dev(z, x, y, k), dev(z, x, y, 1 - k)) for z, x, y, k in ALL]
ACROSS = [(dev(z, x, y, k), dev(z, x, 1 - y, k)) for z, x, y, k in ALL]


def spread_a():
    pairs = []
    for z in range(4):
        for x in range(2):
            pairs.append((dev(z, x, 0, x), dev(z ^ 1, x, z % 2, x)))
            pairs.append((dev(z, x, 0, 1 - x), dev(z ^ 2, x, z % 2, x)))
            pairs.append((dev(z, x, 1, x), dev(z, x, 1, 1 - x)))
            pairs.append((dev(z, x, 1, 1 - x), dev(z, x, 0, 1 - x)))
    return pairs


def spread_b():
    pairs = []
    for z in range(4):
        for x in range(2):
            pairs.append((dev(z, x, 0, x), dev(z ^ 3, x, z % 2, x)))
            if z % 2:
                pairs.append((dev(z, x, 0, 1 - x), dev(z, x, 1, x)))
                pairs.append((dev(z, x, 1, x), dev(z, x, 1, 1 - x)))
                pairs.append((dev(z, x, 1, 1 - x), dev(z, x, 0, 1 - x)))
            else:
                pairs.append((dev(z, x, 0, 1 - x), dev(z, x, 0, x)))
                pairs.append((dev(z, x, 1, x), dev(z, x, 1, 1 - x)))
                pairs.append((dev(z, x, 1, 1 - x), dev(z, x, 0, 1 - x)))
    return pairs


ASIDE = [
    (dev(z, x, y, k), dev(z, 1 - x, y, k) if k == x else dev(z, x, y, 1 - k))
    for z, x, y, k in ALL
]


def send(value, pairs):
    return lax.ppermute(value, AXES, pairs)


def split(value):
    high = value.astype(BF16)
    return high, (value - high.astype(F32)).astype(BF16)


def mul(a, b):
    return jnp.dot(a, b, preferred_element_type=F32)


def solve(rows, lt_hi, lt_lo):
    hi, lo = split(rows)
    return (mul(hi, lt_hi) + (mul(hi, lt_lo) + mul(lo, lt_hi))).astype(BF16)


def early_kernel(c_ref, _, l0, l1, l2, l3, *refs):
    s_ref, hi_ref, lo_ref, lt_ref = refs[-4:]
    c = c_ref[0]
    for i, block in enumerate((l0, l1, l2, l3)):
        at = pl.multiple_of((c ^ i) * 64, 64)
        lt_ref[pl.ds(at, 64), :] = block[...]
    hi, lo = split(lt_ref[...])
    hi_ref[...] = hi
    lo_ref[...] = lo
    for i, rows in enumerate(refs[:-4]):
        s_ref[i] = solve(rows[...], hi, lo)


VMEM = pl.BlockSpec(memory_space=pltpu.VMEM)
SMEM = pl.BlockSpec(memory_space=pltpu.SMEM)
LIMIT = pltpu.CompilerParams(vmem_limit_bytes=24 * 1024 * 1024)


def early(c, trailing, blocks, parts):
    n = parts[0].shape[0]
    return pl.pallas_call(
        early_kernel,
        out_shape=(
            jax.ShapeDtypeStruct((len(parts), n, NB), BF16),
            jax.ShapeDtypeStruct((NB, NB), BF16),
            jax.ShapeDtypeStruct((NB, NB), BF16),
        ),
        in_specs=[SMEM, VMEM] + [VMEM] * (4 + len(parts)),
        out_specs=(VMEM, VMEM, VMEM),
        scratch_shapes=[pltpu.VMEM((NB, NB), F32)],
        compiler_params=LIMIT,
    )(c, trailing, *blocks, *parts)


def late_kernel(hi_ref, lo_ref, *refs):
    hi, lo = hi_ref[...], lo_ref[...]
    for i, rows in enumerate(refs[:-1]):
        refs[-1][i] = solve(rows[...], hi, lo)


def late(hi, lo, parts):
    n = parts[0].shape[0]
    return pl.pallas_call(
        late_kernel,
        out_shape=jax.ShapeDtypeStruct((len(parts), n, NB), BF16),
        in_specs=[VMEM] * (2 + len(parts)),
        out_specs=VMEM,
        compiler_params=LIMIT,
    )(hi, lo, *parts)


def final_kernel(c_ref, t_ref, sa, sb, sc, ta, tb, hi_ref, lo_ref, o_ref, m_ref, buf, sems):
    c = c_ref[0]
    n = buf.shape[1]
    hi, lo = hi_ref[...], lo_ref[...]
    m_ref[:NB] = solve(ta[...], hi, lo)
    m_ref[NB:] = solve(tb[...], hi, lo)
    mirror = m_ref[...]
    copies = []
    for i, (source, part, row) in enumerate(ORDER):
        at = pl.multiple_of((c ^ part) * 2 * n + row * n, n)
        rows = (sa, sb, sc)[source[0]][source[1]]
        update = lax.dot_general(
            rows, mirror, (((1,), (1,)), ((), ())), preferred_element_type=F32
        )
        buf[i] = (t_ref[pl.ds(at, n), :].astype(F32) - update).astype(BF16)
        copy = pltpu.make_async_copy(buf.at[i], o_ref.at[pl.ds(at, n), :], sems.at[i])
        copy.start()
        copies.append(copy)
    for copy in copies:
        copy.wait()


def final(c, trailing, sa, sb, sc, ta, tb, hi, lo):
    rows, cols = trailing.shape
    n = rows // 8
    return pl.pallas_call(
        final_kernel,
        out_shape=jax.ShapeDtypeStruct((rows, cols), BF16),
        in_specs=[SMEM] + [VMEM] * 8,
        out_specs=pl.BlockSpec(memory_space=pl.ANY),
        scratch_shapes=[
            pltpu.VMEM((2 * NB, NB), BF16),
            pltpu.VMEM((8, n, cols), BF16),
            pltpu.SemaphoreType.DMA((8,)),
        ],
        compiler_params=LIMIT,
    )(c, trailing, sa, sb, sc, ta, tb, hi, lo)


def widen(value):
    return value.astype(F32) * (1.0 / SCALE)


def narrow(value):
    return (value * SCALE).astype(F16)


def local_8x4(trailing, panel, diag_inverse):
    row, col = lax.axis_index("row"), lax.axis_index("col")
    z, x, y, k = row // 2, row % 2, col // 2, col % 2
    barrier = lax.optimization_barrier
    c = jnp.full((1,), col, jnp.int32)
    inv = diag_inverse.T

    mate = send(panel, CORE)
    inv_y = send(inv, ACROSS)
    p, m = narrow(panel), narrow(mate)
    top = jnp.where(k == 0, p[:NB], m[:NB])
    p, m, top = barrier((p, m, top))
    y0, y1 = send(p[:NB], ACROSS), send(p[NB:], ACROSS)
    ra, rb = send(top, spread_a()), send(top, spread_b())
    r = jnp.concatenate([ra, rb], 0)
    xr = send(r, ASIDE)
    inv_y, inv, *_ = barrier((inv_y, inv, r))
    y1, *_ = barrier((y1, r))
    inv_k, inv_ky = send(inv, CORE), send(inv_y, CORE)
    ky0, ky1 = send(y0, CORE), send(y1, CORE)
    blocks = (inv, inv_k, inv_y, inv_ky)
    s, hi, lo = early(c, trailing, blocks, [widen(v) for v in (p[:NB], p[NB:], m[:NB], m[NB:])])
    sb = late(hi, lo, [widen(v) for v in (y0, ky0)])
    sc = late(hi, lo, [widen(v) for v in (y1, ky1)])
    xr, _ = barrier((xr, sc))
    sa = s
    here = x == k
    a = jnp.where(here, r[:NB], xr[:NB])
    b = jnp.where(here, r[NB:], xr[NB:])
    a_low = jnp.where(z % 2 == y, z >= 2, z < 2)
    ta = widen(jnp.where(a_low, a, b))
    tb = widen(jnp.where(a_low, b, a))
    return final(c, trailing, sa, sb, sc, ta, tb, hi, lo)


def solution(mesh):
    in_specs = (P("row", "col"), P(("row", "col"), None), P(None, "col"))
    out_specs = P("row", "col")
    fits = mesh.shape["row"] == 8 and mesh.shape["col"] == 4
    return jax.shard_map(
        local_8x4 if fits else local_any,
        mesh=mesh,
        in_specs=in_specs,
        out_specs=out_specs,
        check_vma=False,
    )
```

```python
import jax
import jax.numpy as jnp
from jax import lax
from jax.experimental import pallas as pl
from jax.experimental.pallas import tpu as pltpu
from jax.sharding import PartitionSpec as P

NB = 256
SBLK = 2
SCALE = 32768.0
ORDER = (
    ((0, 0), 0, 0), ((0, 1), 0, 1), ((0, 2), 1, 0), ((0, 3), 1, 1),
    ((1, 0), 2, 0), ((1, 1), 2, 1), ((1, 2), 3, 0), ((1, 3), 3, 1),
)
AXES = ("row", "col")
F32, F16, BF16 = jnp.float32, jnp.float16, jnp.bfloat16


def from_root(value, axis, source):
    kept = jnp.where(lax.axis_index(axis) == source, value, 0).astype(value.dtype)
    return lax.psum(kept, axis)


def solve_rows(rows_in, inverse):
    return lax.dot_general(
        rows_in,
        inverse,
        (((1,), (1,)), ((), ())),
        precision=lax.Precision.HIGHEST,
        preferred_element_type=F32,
    ).astype(BF16)


def local_any(trailing, panel, diag_inverse):
    inverse = lax.all_gather(diag_inverse, "col", axis=1, tiled=True)
    raw_rows = lax.all_gather(panel, "col", axis=0, tiled=True)
    solved = solve_rows(raw_rows, inverse)
    top_block = solved[:NB]
    col_index = lax.axis_index("col")
    col_count = lax.axis_size("col")
    pieces = []
    for section in range(SBLK):
        pieces.append(from_root(top_block, "row", col_index + section * col_count))
    mirror = jnp.concatenate(pieces, 0)
    update = lax.dot_general(
        solved, mirror, (((1,), (1,)), ((), ())), preferred_element_type=F32
    )
    return (trailing.astype(F32) - update).astype(BF16)


def dev(z, x, y, k):
    return (z * 2 + x) * 4 + y * 2 + k


ALL = [(z, x, y, k) for z in range(4) for x in range(2) for y in range(2) for k in range(2)]
CORE = [(dev(z, x, y, k), dev(z, x, y, 1 - k)) for z, x, y, k in ALL]
ACROSS = [(dev(z, x, y, k), dev(z, x, 1 - y, k)) for z, x, y, k in ALL]


def spread_a():
    pairs = []
    for z in range(4):
        for x in range(2):
            pairs.append((dev(z, x, 0, x), dev(z ^ 1, x, z % 2, x)))
            pairs.append((dev(z, x, 0, 1 - x), dev(z ^ 2, x, z % 2, x)))
            pairs.append((dev(z, x, 1, x), dev(z, x, 1, 1 - x)))
            pairs.append((dev(z, x, 1, 1 - x), dev(z, x, 0, 1 - x)))
    return pairs


def spread_b():
    pairs = []
    for z in range(4):
        for x in range(2):
            far = 1 if z % 2 else x
            pairs.append((dev(z, x, 0, far), dev(z ^ 3, x, z % 2, x)))
            if z % 2:
                pairs.append((dev(z, x, 0, 1 - far), dev(z, x, 1, x)))
                pairs.append((dev(z, x, 1, x), dev(z, x, 1, 1 - x)))
                pairs.append((dev(z, x, 1, 1 - x), dev(z, x, 0, 1 - x)))
            else:
                pairs.append((dev(z, x, 0, 1 - x), dev(z, x, 0, x)))
                pairs.append((dev(z, x, 1, x), dev(z, x, 1, 1 - x)))
                pairs.append((dev(z, x, 1, 1 - x), dev(z, x, 0, 1 - x)))
    return pairs


ASIDE = [
    (dev(z, x, y, k), dev(z, 1 - x, y, k) if k == x else dev(z, x, y, 1 - k))
    for z, x, y, k in ALL
]


def send(value, pairs):
    return lax.ppermute(value, AXES, pairs)


def split(value):
    high = value.astype(BF16)
    return high, (value - high.astype(F32)).astype(BF16)


def mul(a, b):
    return jnp.dot(a, b, preferred_element_type=F32)


def solve(rows, lt_hi, lt_lo):
    hi, lo = split(rows)
    return (mul(hi, lt_hi) + (mul(hi, lt_lo) + mul(lo, lt_hi))).astype(BF16)


def early_kernel(c_ref, _, l0, l1, l2, l3, *refs):
    s_ref, hi_ref, lo_ref, lt_ref = refs[-4:]
    c = c_ref[0]
    for i, block in enumerate((l0, l1, l2, l3)):
        at = pl.multiple_of((c ^ i) * 64, 64)
        lt_ref[pl.ds(at, 64), :] = block[...]
    hi, lo = split(lt_ref[...])
    hi_ref[...] = hi
    lo_ref[...] = lo
    for i, rows in enumerate(refs[:-4]):
        s_ref[i] = solve(rows[...], hi, lo)


VMEM = pl.BlockSpec(memory_space=pltpu.VMEM)
SMEM = pl.BlockSpec(memory_space=pltpu.SMEM)
LIMIT = pltpu.CompilerParams(vmem_limit_bytes=24 * 1024 * 1024)


def early(c, trailing, blocks, parts):
    n = parts[0].shape[0]
    return pl.pallas_call(
        early_kernel,
        out_shape=(
            jax.ShapeDtypeStruct((len(parts), n, NB), BF16),
            jax.ShapeDtypeStruct((NB, NB), BF16),
            jax.ShapeDtypeStruct((NB, NB), BF16),
        ),
        in_specs=[SMEM, VMEM] + [VMEM] * (4 + len(parts)),
        out_specs=(VMEM, VMEM, VMEM),
        scratch_shapes=[pltpu.VMEM((NB, NB), F32)],
        compiler_params=LIMIT,
    )(c, trailing, *blocks, *parts)


def late_kernel(hi_ref, lo_ref, *refs):
    hi, lo = hi_ref[...], lo_ref[...]
    for i, rows in enumerate(refs[:-1]):
        refs[-1][i] = solve(rows[...], hi, lo)


def late(hi, lo, parts):
    n = parts[0].shape[0]
    return pl.pallas_call(
        late_kernel,
        out_shape=jax.ShapeDtypeStruct((len(parts), n, NB), BF16),
        in_specs=[VMEM] * (2 + len(parts)),
        out_specs=VMEM,
        compiler_params=LIMIT,
    )(hi, lo, *parts)


def final_kernel(c_ref, t_ref, sa, sb, ta, tb, hi_ref, lo_ref, o_ref, m_ref, buf, sems):
    c = c_ref[0]
    n = buf.shape[1]
    hi, lo = hi_ref[...], lo_ref[...]
    m_ref[:NB] = solve(ta[...], hi, lo)
    m_ref[NB:] = solve(tb[...], hi, lo)
    mirror = m_ref[...]
    copies = []
    for i, (source, part, row) in enumerate(ORDER):
        at = pl.multiple_of((c ^ part) * 2 * n + row * n, n)
        rows = (sa, sb)[source[0]][source[1]]
        update = lax.dot_general(
            rows, mirror, (((1,), (1,)), ((), ())), preferred_element_type=F32
        )
        buf[i] = (t_ref[pl.ds(at, n), :].astype(F32) - update).astype(BF16)
        copy = pltpu.make_async_copy(buf.at[i], o_ref.at[pl.ds(at, n), :], sems.at[i])
        copy.start()
        copies.append(copy)
    for copy in copies:
        copy.wait()


def final(c, trailing, sa, sb, ta, tb, hi, lo):
    rows, cols = trailing.shape
    n = rows // 8
    return pl.pallas_call(
        final_kernel,
        out_shape=jax.ShapeDtypeStruct((rows, cols), BF16),
        in_specs=[SMEM] + [VMEM] * 7,
        out_specs=pl.BlockSpec(memory_space=pl.ANY),
        scratch_shapes=[
            pltpu.VMEM((2 * NB, NB), BF16),
            pltpu.VMEM((8, n, cols), BF16),
            pltpu.SemaphoreType.DMA((8,)),
        ],
        compiler_params=LIMIT,
    )(c, trailing, sa, sb, ta, tb, hi, lo)


def widen(value):
    return value.astype(F32) * (1.0 / SCALE)


def narrow(value):
    return (value * SCALE).astype(F16)


def local_8x4(trailing, panel, diag_inverse):
    row, col = lax.axis_index("row"), lax.axis_index("col")
    z, x, y, k = row // 2, row % 2, col // 2, col % 2
    barrier = lax.optimization_barrier
    c = jnp.full((1,), col, jnp.int32)
    inv = diag_inverse.T

    mate = send(panel, CORE)
    inv_y = send(inv, ACROSS)
    p, m = narrow(panel), narrow(mate)
    top = jnp.where(k == 0, p[:NB], m[:NB])
    p, m, top = barrier((p, m, top))
    y0, y1 = send(p[:NB], ACROSS), send(p[NB:], ACROSS)
    ra, rb = send(top, spread_a()), send(top, spread_b())
    r = jnp.concatenate([ra, rb], 0)
    xr = send(r, ASIDE)
    inv_y, inv, *_ = barrier((inv_y, inv, r))
    y1, *_ = barrier((y1, r))
    inv_k, inv_ky = send(inv, CORE), send(inv_y, CORE)
    ky0, ky1 = send(y0, CORE), send(y1, CORE)
    blocks = (inv, inv_k, inv_y, inv_ky)
    s, hi, lo = early(c, trailing, blocks, [widen(v) for v in (p[:NB], p[NB:], m[:NB], m[NB:])])
    sb = late(hi, lo, [widen(v) for v in (y0, y1, ky0, ky1)])
    xr, _ = barrier((xr, sb))
    sa = s
    here = x == k
    a = jnp.where(here, r[:NB], xr[:NB])
    b = jnp.where(here, r[NB:], xr[NB:])
    a_low = jnp.where(z % 2 == y, z >= 2, z < 2)
    ta = widen(jnp.where(a_low, a, b))
    tb = widen(jnp.where(a_low, b, a))
    return final(c, trailing, sa, sb, ta, tb, hi, lo)


def solution(mesh):
    in_specs = (P("row", "col"), P(("row", "col"), None), P(None, "col"))
    out_specs = P("row", "col")
    fits = mesh.shape["row"] == 8 and mesh.shape["col"] == 4
    return jax.shard_map(
        local_8x4 if fits else local_any,
        mesh=mesh,
        in_specs=in_specs,
        out_specs=out_specs,
        check_vma=False,
    )
```
